256 devices in a mesh: row: 32 (over x, z_lo, core), col: 8 (over z_hi, y).
Axes of the slice: x: 4, y: 4, z: 8 (z_hi: 2, z_lo: 4; z = z_hi * 4 + z_lo), core: 2. Of those that a mesh axis runs over, the one named last changes fastest.
Arguments:
- features: bfloat16 [32768, 128], P(('col', 'row')), may hold values from -6 to 6
- block_values: bfloat16 [36864, 128, 128], P(('row', 'col')), may hold values from -0.25 to 0.25
- block_slots: int32 [36864], P(('row', 'col')), may hold values from 0 to 255, as said below
- block_counts: int32 [256], P(('row', 'col')), may hold values from 48 to 144, as said below
- w_in: bfloat16 [128, 256], replicated, may hold values from -0.5 to 0.5
- w_out: bfloat16 [256, 172], replicated, may hold values from -0.375 to 0.375
- logit_grad: bfloat16 [32768, 172], P(('col', 'row')), may hold values from -0.032958984 to 0.032958984
Outputs:
- logits: bfloat16 [32768, 172], P(('col', 'row'))
- w_in_grad: float32 [128, 256], replicated
- w_out_grad: float32 [256, 172], replicated
The draws below stay inside these ranges and needn't reach their ends.
Inputs may be any that keep to these rules, and one draw needn't show every extreme that they name: `block_slots`: within each tile's 144 entries the slots are distinct; slot s is block row s // 8 and block column s % 8 of the tile. The first block_counts[t] blocks of tile t are live, the others are padding; some tile is full.
All inputs are finite; a program needn't handle non-finite values.
Results may differ from the reference program's by a relative error of at most 0.0071.
Values may be sent and summed in bfloat16 or wider, within the bound.
No kernel may reach another device: no remote copies, remote signals or barrier semaphores. Data moves between devices by JAX's collectives and lax.ppermute only.
A program may use at most 128 MiB of HBM per device.

```python
import jax
import jax.numpy as jnp
from jax import lax

FIN = 128
HID = 256
CLS = 172
BS = 128
ND = 128
N = 32768
RB = 32
CB = 8
BLK_DEV = 144
TOTAL_BLK = 36864
N_ROW = 32
N_COL = 8


def draw_block_slots(key, part):
    key = jax.random.fold_in(key, 11)
    tile_keys = jax.random.split(key, N_ROW * N_COL)

    def choose_slots(sub_key):
        return jax.random.permutation(sub_key, RB * CB)[:BLK_DEV]
    chosen = jax.vmap(choose_slots)(tile_keys)
    return chosen.reshape(N_ROW * N_COL * BLK_DEV).astype(jnp.int32)


def draw_block_counts(key, part):
    key = jax.random.fold_in(key, 23)
    first_key, second_key = jax.random.split(key)
    counts = jax.random.randint(first_key, (N_ROW * N_COL,), max(1, BLK_DEV // 3), BLK_DEV + 1)
    fullest = jax.random.randint(second_key, (), 0, N_ROW * N_COL)
    filled = jnp.where(jnp.arange(N_ROW * N_COL) == fullest, BLK_DEV, counts)
    return filled.astype(jnp.int32)


def levels(stream_key, shape, pieces, least, top_value):
    gain = 1.0
    for axis_at, blocks in pieces:
        draws = jax.random.uniform(jax.random.fold_in(jax.random.fold_in(stream_key, 6), axis_at), (blocks,), jnp.float32, least / len(pieces), top_value / len(pieces))
        gain = gain * jnp.repeat(jnp.exp(draws), shape[axis_at] // blocks).reshape((-1,) + (1,) * (len(shape) - 1 - axis_at))
    return gain


def noise(rng, shape, scale, reach, cuts=(), kind=jnp.bfloat16):
    result = scale * jax.random.normal(rng, shape, jnp.float32)
    if cuts:
        result = result * levels(rng, shape, cuts, -0.22, 0.18)
    return jnp.clip(result, -reach, reach).astype(kind)


def setup_inputs(seed: int = 0) -> dict:
    splits = jax.random.split(jax.random.key(seed), 8)
    features = noise(splits[0], (N, FIN), 1.0, 6.0, ((0, 256),))
    block_values = noise(splits[1], (TOTAL_BLK, BS, BS), (BS * max(1, BLK_DEV // RB)) ** -0.5, 0.25, ((0, 256),))
    block_slots = draw_block_slots(jax.random.fold_in(splits[7], 71), 0)
    block_counts = draw_block_counts(jax.random.fold_in(splits[7], 71), 0)
    w_in = noise(splits[4], (FIN, HID), FIN ** -0.5, 0.5)
    w_out = noise(splits[5], (HID, CLS), HID ** -0.5, 0.375)
    logit_grad = noise(splits[6], (N, CLS), (N ** -0.5), 0.032958984, ((0, 256),))
    return {"features": features, "block_values": block_values, "block_slots": block_slots, "block_counts": block_counts, "w_in": w_in, "w_out": w_out, "logit_grad": logit_grad}


def aggregate(block_values, block_slots, block_counts, feats, transpose):
    block_total = N // BS
    feature_width = feats.shape[1]
    feat_blocks = feats.astype(jnp.float32).reshape(block_total, BS, feature_width)
    value_blocks = block_values.reshape(N_ROW * N_COL, BLK_DEV, BS, BS)
    slot_table = block_slots.reshape(N_ROW * N_COL, BLK_DEV)
    positions = jnp.arange(BLK_DEV, dtype=jnp.int32)

    def one_tile(device, summed):
        row_pos = device // N_COL
        col_pos = device % N_COL
        slot_ids = slot_table[device]
        alive_mask = (positions < block_counts[device]).astype(jnp.float32)
        tile_blocks = value_blocks[device].astype(jnp.float32) * alive_mask[:, None, None]
        dst_block = col_pos * RB + slot_ids // CB
        first_col = slot_ids % CB * BS
        src_block = ((first_col // ND * N_ROW + row_pos) * ND + first_col % ND) // BS
        if transpose:
            products = jnp.einsum('bji,bjf->bif', tile_blocks, feat_blocks[dst_block], precision=lax.Precision.HIGHEST)
            return summed.at[src_block].add(products)
        products = jnp.einsum('bij,bjf->bif', tile_blocks, feat_blocks[src_block], precision=lax.Precision.HIGHEST)
        return summed.at[dst_block].add(products)
    start_sum = jnp.zeros((block_total, BS, feature_width), jnp.float32)
    summed = lax.fori_loop(0, N_ROW * N_COL, one_tile, start_sum)
    return summed.reshape(N, feature_width)

def reference(features, block_values, block_slots, block_counts, w_in, w_out, logit_grad):
    aggregated = aggregate(block_values, block_slots, block_counts, features, False).astype(jnp.bfloat16)
    pre_act = jnp.dot(aggregated, w_in, preferred_element_type=jnp.float32)
    hidden = jax.nn.silu(pre_act).astype(jnp.bfloat16)
    mixed = aggregate(block_values, block_slots, block_counts, hidden, False)
    w_out_wide = w_out.astype(jnp.float32)
    logits = jnp.dot(mixed, w_out_wide, precision=lax.Precision.HIGHEST).astype(jnp.bfloat16)
    w_out_grad = jnp.dot(mixed.T, logit_grad.astype(jnp.float32), precision=lax.Precision.HIGHEST)
    back_rows = jnp.dot(logit_grad, w_out.T, preferred_element_type=jnp.float32)
    spread = aggregate(block_values, block_slots, block_counts, back_rows, True)
    _, pullback = jax.vjp(jax.nn.silu, pre_act)
    pre_grad = pullback(spread)[0].astype(jnp.bfloat16)
    w_in_grad = jnp.dot(aggregated.T, pre_grad, preferred_element_type=jnp.float32)
    return (logits, w_in_grad, w_out_grad)
```

```python
import functools

import jax
import jax.numpy as jnp
from jax import lax
from jax.experimental import pallas as pl
from jax.experimental.pallas import tpu as pltpu
from jax.sharding import PartitionSpec as P

F32 = jnp.float32
BF16 = jnp.bfloat16
BS = 128
CLSP = 176
UNIT = 16
UNITS = 10
SHARE = UNITS * UNIT
VMEM_LIMIT = 48 * 1024 * 1024
STEP = 512


def vmem():
    return pl.BlockSpec(memory_space=pltpu.VMEM)


def smem():
    return pl.BlockSpec(memory_space=pltpu.SMEM)


def dot(a, b, da, db):
    return lax.dot_general(a, b, (((da,), (db,)), ((), ())), preferred_element_type=F32)


def call(body, outs, args, specs=None, scratch=(), flops=0):
    return pl.pallas_call(
        body,
        out_shape=[o if len(o) == 1 else jax.ShapeDtypeStruct(*o) for o in outs],
        in_specs=specs or [vmem()] * len(args),
        out_specs=[vmem()] * len(outs),
        scratch_shapes=scratch,
        compiler_params=pltpu.CompilerParams(vmem_limit_bytes=VMEM_LIMIT),
        cost_estimate=pl.CostEstimate(flops=flops, bytes_accessed=2**20, transcendentals=0),
    )(*args)


def densify_body(me_ref, count_ref, slot_ref, block_ref, dense_ref):
    dense_ref[...] = jnp.zeros_like(dense_ref)
    me = me_ref[0]

    def place(b, carry):
        slot = slot_ref[b]
        rel = lax.bitwise_xor(slot // 8, me)
        at = (rel % 2) * 16 + rel // 2
        row = pl.multiple_of(at * BS, BS)
        col = pl.multiple_of((slot % 8) * BS, BS)
        dense_ref[pl.ds(row, BS), pl.ds(col, BS)] = block_ref[b]
        return carry

    lax.fori_loop(0, count_ref[0], place, 0)


def densify(me, counts, slots, blocks):
    return call(
        densify_body,
        [((4096, 1024), BF16)],
        (me, counts, slots, blocks),
        [smem(), smem(), smem(), vmem()],
    )[0]


def hbm():
    return pl.BlockSpec(memory_space=pl.ANY)


def stage(chunks):
    return [pltpu.VMEM((chunks, STEP, 1024), BF16), pltpu.SemaphoreType.DMA((chunks,))]


def copies(dense_ref, buffer_ref, sem_ref, first, chunks):
    return [
        pltpu.make_async_copy(
            dense_ref.at[pl.ds((first + i) * STEP, STEP)], buffer_ref.at[i], sem_ref.at[i]
        )
        for i in range(chunks)
    ]


def rows_product_body(half, dense_ref, right_ref, out_ref, buffer_ref, sem_ref):
    moves = copies(dense_ref, buffer_ref, sem_ref, 4 * half, 4)
    for move in moves:
        move.start()
    right = right_ref[...]
    for i, move in enumerate(moves):
        move.wait()
        out_ref[i * STEP : (i + 1) * STEP, :] = dot(buffer_ref[i], right, 1, 0).astype(out_ref.dtype)


def rows_product(dense, right, half, dtype):
    return call(
        functools.partial(rows_product_body, half),
        [((2048, BS), dtype)],
        (dense, right),
        [hbm(), vmem()],
        stage(4),
        flops=2 * 2048 * 1024 * 256,
    )[0]


def class_rows(wide, moves, buffer_ref, out_ref):
    for i, move in enumerate(moves):
        move.wait()
        part = dot(wide, buffer_ref[i], 1, 1).astype(out_ref.dtype)
        for j in range(4):
            at = (i * 4 + j) * CLSP
            out_ref[at : at + CLSP, :] = part[:, j * BS : (j + 1) * BS]


def silu_inputs(agg_ref, w_in_ref):
    pre = dot(agg_ref[...], w_in_ref[...], 1, 0)
    gate = 1.0 / (1.0 + jnp.exp(-pre))
    return pre, gate, (pre * gate).astype(BF16)


def add_grads(pre, gate, hid, agg, q, w_out, x, out_ref):
    high = q.astype(BF16)
    low = (q - high.astype(F32)).astype(BF16)
    spread = dot(high, w_out, 0, 0) + dot(low, w_out, 0, 0)
    pre_grad = (spread * (gate * (1.0 + pre * (1.0 - gate)))).astype(BF16)
    in_grad = dot(agg, pre_grad, 0, 0)
    out_grad = dot(high, hid, 1, 0) + dot(low, hid, 1, 0)
    pieces = []
    for array in (in_grad, out_grad):
        rows = array.shape[0]
        over = -rows % UNIT
        if over:
            array = jnp.concatenate([array, jnp.zeros((over, array.shape[1]), F32)])
        array = array.astype(BF16)
        for side in range(2):
            pieces.append(array[:, side * BS : (side + 1) * BS])
    used = sum(piece.shape[0] for piece in pieces)
    pieces.append(jnp.zeros((4 * SHARE - used, BS), BF16))
    flat = jnp.concatenate(pieces)
    for j in range(4):
        at = pl.multiple_of(16 * CLSP + lax.bitwise_xor(j, x) * SHARE, UNIT)
        out_ref[pl.ds(at, SHARE), :] = flat[j * SHARE : (j + 1) * SHARE, :]


def class_rows_far_body(
    agg_ref, w_in_ref, w_out_ref, q_ref, me_ref, dense_ref, wide_ref, out_ref, buffer_ref, sem_ref
):
    moves = copies(dense_ref, buffer_ref, sem_ref, 4, 4)
    for move in moves:
        move.start()
    pre, gate, hid = silu_inputs(agg_ref, w_in_ref)
    wide = dot(w_out_ref[...], hid, 1, 1)
    zeros = jnp.zeros((CLSP - wide.shape[0], wide.shape[1]), F32)
    wide_ref[...] = jnp.concatenate([wide, zeros]).astype(BF16)
    class_rows(wide_ref[...], moves, buffer_ref, out_ref)
    add_grads(pre, gate, hid, agg_ref[...], q_ref[...], w_out_ref[...], me_ref[0] // 8, out_ref)


def class_rows_far(agg, w_in, w_out_t, q, me, dense):
    return call(
        class_rows_far_body,
        [((CLSP, 1024), BF16), ((16 * CLSP + 4 * SHARE, BS), BF16)],
        (agg, w_in, w_out_t, q, me, dense),
        [vmem(), vmem(), vmem(), vmem(), smem(), hbm()],
        stage(4),
        flops=4 * 2048 * 1024 * 256,
    )


def class_rows_near_body(wide_ref, dense_ref, out_ref, buffer_ref, sem_ref):
    moves = copies(dense_ref, buffer_ref, sem_ref, 0, 4)
    for move in moves:
        move.start()
    class_rows(wide_ref[...], moves, buffer_ref, out_ref)


def class_rows_near(wide, dense):
    return call(
        class_rows_near_body,
        [((16 * CLSP, BS), F32)],
        (wide, dense),
        [vmem(), hbm()],
        stage(4),
        flops=2 * 2048 * 1024 * 256,
    )[0]


def class_columns_body(near_ref, far_ref, dense_ref, out_ref, buffer_ref, sem_ref):
    moves = copies(dense_ref, buffer_ref, sem_ref, 0, 8)
    for move in moves:
        move.start()
    for i, move in enumerate(moves):
        ref = near_ref if i < 4 else far_ref
        left = jnp.concatenate([ref[(i % 4) * 4 + j] for j in range(4)], axis=1)
        move.wait()
        part = dot(left, buffer_ref[i], 1, 0)
        if i == 0:
            out_ref[...] = part
        else:
            out_ref[...] += part


def class_columns(near, far, dense):
    return call(
        class_columns_body,
        [((near.shape[1], 1024), F32)],
        (near, far, dense),
        [vmem(), vmem(), hbm()],
        stage(8),
        flops=2 * 4096 * 1024 * 256,
    )[0]


def copies_body(features_ref, send_ref):
    for c in range(8):
        send_ref[c] = features_ref[...]


def eight_copies(features):
    return call(copies_body, [((8, BS, BS), BF16)], (features,))[0]


def core_sum_body(mine_ref, got_ref, s1_ref, s2_ref, s3_ref, keep_ref):
    n = keep_ref.shape[0]
    for d, ref in ((1, s1_ref), (2, s2_ref), (3, s3_ref), (0, keep_ref)):
        at = slice(d * n, (d + 1) * n)
        ref[...] = (mine_ref[at, :].astype(F32) + got_ref[at, :].astype(F32)).astype(ref.dtype)


def core_sum(mine, got):
    rows = mine.shape[0] // 4
    shape = (rows, BS)
    return call(core_sum_body, [(shape, BF16)] * 3 + [(shape, F32)], (mine, got))


def four(a, b, c, d):
    return (a.astype(F32) + b.astype(F32)) + (c.astype(F32) + d.astype(F32))


def x_sum_body(keep_ref, r1_ref, r2_ref, r3_ref, s1_ref, s2_ref, s3_ref, out_ref):
    n = out_ref.shape[0]
    for d, ref in ((1, s1_ref), (2, s2_ref), (3, s3_ref), (0, out_ref)):
        at = slice(d * n, (d + 1) * n)
        total = four(keep_ref[at, :], r1_ref[at, :], r2_ref[at, :], r3_ref[at, :])
        ref[...] = total.astype(ref.dtype)


def x_sum(keep, received):
    shape = (keep.shape[0] // 4, BS)
    return call(x_sum_body, [(shape, BF16)] * 3 + [(shape, F32)], (keep, *received))


def core_sum_grad_body(mine_ref, far_ref, got_ref, s1_ref, s2_ref, s3_ref, keep_ref):
    n = 4 * CLSP
    for d, ref in ((1, s1_ref), (2, s2_ref), (3, s3_ref), (0, keep_ref)):
        at = slice(d * n, (d + 1) * n)
        ref[:n, :] = (mine_ref[at, :].astype(F32) + got_ref[at, :].astype(F32)).astype(ref.dtype)
        at = slice(4 * n + d * SHARE, 4 * n + (d + 1) * SHARE)
        ref[n:, :] = (far_ref[at, :].astype(F32) + got_ref[at, :].astype(F32)).astype(ref.dtype)


def core_sum_grad(mine, far, got):
    shape = (4 * CLSP + SHARE, BS)
    return call(core_sum_grad_body, [(shape, BF16)] * 3 + [(shape, F32)], (mine, far, got))


def x_sum_grad_body(keep_ref, r1_ref, r2_ref, r3_ref, s1_ref, s2_ref, s3_ref, out_ref):
    n = CLSP
    tail = slice(4 * n, 4 * n + SHARE)
    share = four(keep_ref[tail, :], r1_ref[tail, :], r2_ref[tail, :], r3_ref[tail, :])
    for d, ref in ((1, s1_ref), (2, s2_ref), (3, s3_ref), (0, out_ref)):
        at = slice(d * n, (d + 1) * n)
        total = four(keep_ref[at, :], r1_ref[at, :], r2_ref[at, :], r3_ref[at, :])
        ref[:n, :] = total.astype(ref.dtype)
        ref[n:, :] = share.astype(BF16).astype(ref.dtype)


def x_sum_grad(keep, received):
    shape = (CLSP + SHARE, BS)
    return call(x_sum_grad_body, [(shape, BF16)] * 3 + [(shape, F32)], (keep, *received))


def z_sum_grad_body(keep_ref, r1_ref, r2_ref, r3_ref, logit_ref, share_ref):
    total = four(keep_ref[...], r1_ref[...], r2_ref[...], r3_ref[...])
    logit_ref[...] = total[: logit_ref.shape[0], :].astype(BF16)
    for c in range(8):
        share_ref[c] = total[CLSP:, :].astype(BF16)


def z_sum_grad(keep, received, classes):
    return call(
        z_sum_grad_body,
        [((classes, BS), BF16), ((8, SHARE, BS), BF16)],
        (keep, *received),
    )


def aggregate_body(keep_ref, r1_ref, r2_ref, r3_ref, send_ref):
    agg = four(keep_ref[...], r1_ref[...], r2_ref[...], r3_ref[...]).astype(BF16)
    for c in range(8):
        send_ref[c] = agg


def aggregate(keep, received):
    return call(aggregate_body, [((8, BS, BS), BF16)], (keep, *received))[0]


def share_sum_body(parts_ref, out_ref):
    total = parts_ref[0].astype(F32)
    for c in range(1, 8):
        total = total + parts_ref[c].astype(F32)
    out_ref[...] = total


def share_sum(parts):
    return call(share_sum_body, [((SHARE, BS), F32)], (parts,))[0]


def unpack_body(me_ref, own_ref, r1_ref, r2_ref, r3_ref, in_ref, out_ref, all_ref):
    x = me_ref[0] // 8
    for d, ref in enumerate((own_ref, r1_ref, r2_ref, r3_ref)):
        all_ref[lax.bitwise_xor(d, x)] = ref[...]
    unit = 0
    for ref in (in_ref, out_ref):
        for side in range(2):
            for u in range(-(-ref.shape[0] // UNIT)):
                place, at = divmod(unit, UNITS)
                rows = min(UNIT, ref.shape[0] - u * UNIT)
                ref[u * UNIT : u * UNIT + rows, side * BS : (side + 1) * BS] = all_ref[
                    place, at * UNIT : at * UNIT + rows, :
                ]
                unit += 1


def unpack(me, own, received, classes):
    return call(
        unpack_body,
        [((128, 256), F32), ((classes, 256), F32)],
        (me, own, *received),
        [smem()] + [vmem()] * 4,
        [pltpu.VMEM((4, SHARE, BS), F32)],
    )


def permute(x, flip):
    return lax.ppermute(x, "row", [(i, i ^ flip) for i in range(32)])


CORE = 1
Z_FLIPS = (2, 4, 6)
X_FLIPS = (8, 16, 24)


def on_device(features, block_values, block_slots, block_counts, w_in, w_out, logit_grad):
    classes = logit_grad.shape[1]
    me = lax.axis_index("row").astype(jnp.int32).reshape(1)
    w_out_t = w_out.T
    feature_parts = lax.all_to_all(eight_copies(features), "col", 0, 0).reshape(1024, BS)
    dense = densify(me, block_counts, block_slots, block_values)
    grad_t = logit_grad.T
    grad_z = jnp.stack([grad_t] + [permute(grad_t, f) for f in Z_FLIPS])
    grad_near = jnp.concatenate([grad_z] + [permute(grad_z, f) for f in X_FLIPS])
    grad_far = permute(grad_near, CORE)

    far = rows_product(dense, feature_parts, 1, F32)
    got = permute(far, CORE)
    mine = rows_product(dense, feature_parts, 0, F32)
    s1, s2, s3, keep = core_sum(mine, got)
    s1, s2, s3, keep = x_sum(keep, [permute(s, f) for s, f in zip((s1, s2, s3), X_FLIPS)])
    received = [permute(s, f) for s, f in zip((s1, s2, s3), Z_FLIPS)]
    q = class_columns(grad_near, grad_far, dense)
    agg = lax.all_to_all(aggregate(keep, received), "col", 0, 0).reshape(1024, BS)

    wide, far = class_rows_far(agg, w_in, w_out_t, q, me, dense)
    got = permute(far, CORE)
    mine = class_rows_near(wide, dense)
    s1, s2, s3, keep = core_sum_grad(mine, far, got)
    s1, s2, s3, keep = x_sum_grad(keep, [permute(s, f) for s, f in zip((s1, s2, s3), X_FLIPS)])
    received = [permute(s, f) for s, f in zip((s1, s2, s3), Z_FLIPS)]
    logits_t, shares = z_sum_grad(keep, received, classes)
    own = share_sum(lax.all_to_all(shares, "col", 0, 0))
    in_grad, out_grad_t = unpack(me, own, [permute(own, f) for f in X_FLIPS], classes)
    return (logits_t.T, in_grad, out_grad_t.T)


def solution(mesh):
    return jax.shard_map(
        on_device,
        mesh=mesh,
        in_specs=(
            P(("col", "row"), None),
            P(("row", "col"), None, None),
            P(("row", "col")),
            P(("row", "col")),
            P(),
            P(),
            P(("col", "row"), None),
        ),
        out_specs=(P(("col", "row"), None), P(), P()),
        check_vma=False,
    )
```

```python
import functools

import jax
import jax.numpy as jnp
from jax import lax
from jax.experimental import pallas as pl
from jax.experimental.pallas import tpu as pltpu
from jax.sharding import PartitionSpec as P

F32 = jnp.float32
BF16 = jnp.bfloat16
BS = 128
CLSP = 176
UNIT = 16
UNITS = 10
SHARE = UNITS * UNIT
VMEM_LIMIT = 32 * 1024 * 1024
STEP = 512
LOADS = 3
LOAD = 48


def vmem():
    return pl.BlockSpec(memory_space=pltpu.VMEM)


def smem():
    return pl.BlockSpec(memory_space=pltpu.SMEM)


def dot(a, b, da, db):
    return lax.dot_general(a, b, (((da,), (db,)), ((), ())), preferred_element_type=F32)


def call(body, outs, args, specs=None, scratch=(), flops=0):
    return pl.pallas_call(
        body,
        out_shape=[o if len(o) == 1 else jax.ShapeDtypeStruct(*o) for o in outs],
        in_specs=specs or [vmem()] * len(args),
        out_specs=[vmem()] * len(outs),
        scratch_shapes=scratch,
        compiler_params=pltpu.CompilerParams(vmem_limit_bytes=VMEM_LIMIT),
        cost_estimate=pl.CostEstimate(flops=flops, bytes_accessed=2**20, transcendentals=0),
    )(*args)


def hbm():
    return pl.BlockSpec(memory_space=pl.ANY)


def rows_of(dense_ref, first, i):
    at = (first + i) * STEP
    return dense_ref[at : at + STEP, :]


def densify_body(
    me_ref, side_ref, count_ref, slot_ref, block_ref, g0_ref, g1_ref, g2_ref, g3_ref,
    dense_ref, near_ref, held_ref, sem_ref,
):
    moves = [
        pltpu.make_async_copy(
            block_ref.at[pl.ds(i * LOAD, LOAD)], held_ref.at[pl.ds(i * LOAD, LOAD)], sem_ref.at[i]
        )
        for i in range(LOADS)
    ]
    for move in moves:
        move.start()
    dense_ref[...] = jnp.zeros_like(dense_ref)
    for d, ref in enumerate((g0_ref, g1_ref, g2_ref, g3_ref)):
        near_ref[d] = ref[...]
    me = me_ref[0]
    side = side_ref[0]
    count = count_ref[0]

    def place(b, carry):
        slot = slot_ref[b]
        rel = lax.bitwise_xor(slot // 8, me)
        at = (rel % 2) * 16 + rel // 2
        across = lax.bitwise_xor(slot % 8, side)
        row = pl.multiple_of(at * BS, BS)
        col = pl.multiple_of(((across % 4) * 2 + across // 4) * BS, BS)
        dense_ref[pl.ds(row, BS), pl.ds(col, BS)] = held_ref[b]
        return carry

    for i, move in enumerate(moves):
        move.wait()
        lax.fori_loop(i * LOAD, jnp.clip(count, i * LOAD, (i + 1) * LOAD), place, 0)


def densify(me, side, counts, slots, blocks, cotangents):
    return pl.pallas_call(
        densify_body,
        out_shape=[
            pltpu.VMEM((4096, 1024), BF16),
            jax.ShapeDtypeStruct((4,) + cotangents[0].shape, BF16),
        ],
        in_specs=[smem(), smem(), smem(), smem(), hbm()] + [vmem()] * 4,
        out_specs=[vmem(), vmem()],
        scratch_shapes=[pltpu.VMEM(blocks.shape, BF16), pltpu.SemaphoreType.DMA((LOADS,))],
        compiler_params=pltpu.CompilerParams(vmem_limit_bytes=52 * 1024 * 1024),
    )(me, side, counts, slots, blocks, *cotangents)


def joined(refs):
    return jnp.concatenate([ref[h] for ref in refs for h in range(2)])


def rows_product_body(half, dense_ref, r0_ref, r1_ref, r2_ref, r3_ref, out_ref):
    right = joined((r0_ref, r1_ref, r2_ref, r3_ref))
    for i in range(4):
        part = dot(rows_of(dense_ref, 4 * half, i), right, 1, 0)
        out_ref[i * STEP : (i + 1) * STEP, :] = part.astype(out_ref.dtype)


def rows_product(dense, parts, half, dtype):
    return call(
        functools.partial(rows_product_body, half),
        [((2048, BS), dtype)],
        (dense, *parts),
        [vmem()] * 5,
        flops=2 * 2048 * 1024 * 256,
    )[0]


def class_rows(wide, dense_ref, first, out_ref):
    for i in range(4):
        part = dot(wide, rows_of(dense_ref, first, i), 1, 1).astype(out_ref.dtype)
        for j in range(4):
            at = (i * 4 + j) * CLSP
            out_ref[at : at + CLSP, :] = part[:, j * BS : (j + 1) * BS]


def silu_inputs(agg, w_in_ref):
    pre = dot(agg, w_in_ref[...], 1, 0)
    gate = 1.0 / (1.0 + jnp.exp(-pre))
    return pre, gate, (pre * gate).astype(BF16)


def add_grads(pre, gate, hid, agg, q, w_out, x, out_ref):
    high = q.astype(BF16)
    low = (q - high.astype(F32)).astype(BF16)
    spread = dot(high, w_out, 0, 0) + dot(low, w_out, 0, 0)
    pre_grad = (spread * (gate * (1.0 + pre * (1.0 - gate)))).astype(BF16)
    in_grad = dot(agg, pre_grad, 0, 0)
    out_grad = dot(high, hid, 1, 0) + dot(low, hid, 1, 0)
    pieces = []
    for array in (in_grad, out_grad):
        rows = array.shape[0]
        over = -rows % UNIT
        if over:
            array = jnp.concatenate([array, jnp.zeros((over, array.shape[1]), F32)])
        array = array.astype(BF16)
        for side in range(2):
            pieces.append(array[:, side * BS : (side + 1) * BS])
    used = sum(piece.shape[0] for piece in pieces)
    pieces.append(jnp.zeros((4 * SHARE - used, BS), BF16))
    flat = jnp.concatenate(pieces)
    for j in range(4):
        at = pl.multiple_of(16 * CLSP + lax.bitwise_xor(j, x) * SHARE, UNIT)
        out_ref[pl.ds(at, SHARE), :] = flat[j * SHARE : (j + 1) * SHARE, :]


def class_rows_far_body(
    a0_ref, a1_ref, a2_ref, a3_ref, w_in_ref, w_out_ref, q_ref, me_ref, dense_ref,
    wide_ref, out_ref,
):
    agg = joined((a0_ref, a1_ref, a2_ref, a3_ref))
    pre, gate, hid = silu_inputs(agg, w_in_ref)
    wide = dot(w_out_ref[...], hid, 1, 1)
    zeros = jnp.zeros((CLSP - wide.shape[0], wide.shape[1]), F32)
    wide_ref[...] = jnp.concatenate([wide, zeros]).astype(BF16)
    class_rows(wide_ref[...], dense_ref, 4, out_ref)
    add_grads(pre, gate, hid, agg, q_ref[...], w_out_ref[...], me_ref[0] // 8, out_ref)


def class_rows_far(agg, w_in, w_out_t, q, me, dense):
    return call(
        class_rows_far_body,
        [((CLSP, 1024), BF16), ((16 * CLSP + 4 * SHARE, BS), BF16)],
        (*agg, w_in, w_out_t, q, me, dense),
        [vmem()] * 7 + [smem(), vmem()],
        flops=4 * 2048 * 1024 * 256,
    )


def class_rows_near_body(wide_ref, dense_ref, out_ref):
    class_rows(wide_ref[...], dense_ref, 0, out_ref)


def class_rows_near(wide, dense):
    return call(
        class_rows_near_body,
        [((16 * CLSP, BS), F32)],
        (wide, dense),
        flops=2 * 2048 * 1024 * 256,
    )[0]


def class_columns_body(near_ref, far_ref, dense_ref, out_ref):
    for i in range(8):
        ref = near_ref if i < 4 else far_ref
        left = jnp.concatenate([ref[(i % 4) * 4 + j] for j in range(4)], axis=1)
        part = dot(left, rows_of(dense_ref, 0, i), 1, 0)
        if i == 0:
            out_ref[...] = part
        else:
            out_ref[...] += part


def class_columns(near, far, dense):
    return call(
        class_columns_body,
        [((near.shape[1], 1024), F32)],
        (near, far, dense),
        flops=2 * 4096 * 1024 * 256,
    )[0]


def core_sum_body(
    mine_ref, got_ref, g0_ref, g1_ref, g2_ref, g3_ref, s1_ref, s2_ref, s3_ref, keep_ref, near_ref
):
    n = keep_ref.shape[0]
    for d, ref in ((1, s1_ref), (2, s2_ref), (3, s3_ref), (0, keep_ref)):
        at = slice(d * n, (d + 1) * n)
        ref[...] = (mine_ref[at, :].astype(F32) + got_ref[at, :].astype(F32)).astype(ref.dtype)
    for d, ref in enumerate((g0_ref, g1_ref, g2_ref, g3_ref)):
        near_ref[4 * d : 4 * d + 4] = ref[...]


def core_sum(mine, got, cotangents):
    rows = mine.shape[0] // 4
    shape = (rows, BS)
    near = (16,) + cotangents[0].shape[1:]
    return call(
        core_sum_body,
        [(shape, BF16)] * 3 + [(shape, F32), (near, BF16)],
        (mine, got, *cotangents),
    )


def four(a, b, c, d):
    return (a.astype(F32) + b.astype(F32)) + (c.astype(F32) + d.astype(F32))


def x_sum_body(keep_ref, r1_ref, r2_ref, r3_ref, s1_ref, s2_ref, s3_ref, out_ref):
    n = out_ref.shape[0]
    for d, ref in ((1, s1_ref), (2, s2_ref), (3, s3_ref), (0, out_ref)):
        at = slice(d * n, (d + 1) * n)
        total = four(keep_ref[at, :], r1_ref[at, :], r2_ref[at, :], r3_ref[at, :])
        ref[...] = total.astype(ref.dtype)


def x_sum(keep, received):
    shape = (keep.shape[0] // 4, BS)
    return call(x_sum_body, [(shape, BF16)] * 3 + [(shape, F32)], (keep, *received))


def core_sum_grad_body(mine_ref, far_ref, got_ref, s1_ref, s2_ref, s3_ref, keep_ref):
    n = 4 * CLSP
    for d, ref in ((1, s1_ref), (2, s2_ref), (3, s3_ref), (0, keep_ref)):
        at = slice(d * n, (d + 1) * n)
        ref[:n, :] = (mine_ref[at, :].astype(F32) + got_ref[at, :].astype(F32)).astype(ref.dtype)
        at = slice(4 * n + d * SHARE, 4 * n + (d + 1) * SHARE)
        ref[n:, :] = (far_ref[at, :].astype(F32) + got_ref[at, :].astype(F32)).astype(ref.dtype)


def core_sum_grad(mine, far, got):
    shape = (4 * CLSP + SHARE, BS)
    return call(core_sum_grad_body, [(shape, BF16)] * 3 + [(shape, F32)], (mine, far, got))


def x_sum_grad_body(keep_ref, r1_ref, r2_ref, r3_ref, s1_ref, s2_ref, s3_ref, out_ref):
    n = CLSP
    tail = slice(4 * n, 4 * n + SHARE)
    share = four(keep_ref[tail, :], r1_ref[tail, :], r2_ref[tail, :], r3_ref[tail, :])
    for d, ref in ((1, s1_ref), (2, s2_ref), (3, s3_ref), (0, out_ref)):
        at = slice(d * n, (d + 1) * n)
        total = four(keep_ref[at, :], r1_ref[at, :], r2_ref[at, :], r3_ref[at, :])
        ref[:n, :] = total.astype(ref.dtype)
        ref[n:, :] = share.astype(BF16).astype(ref.dtype)


def x_sum_grad(keep, received):
    shape = (CLSP + SHARE, BS)
    return call(x_sum_grad_body, [(shape, BF16)] * 3 + [(shape, F32)], (keep, *received))


def z_sum_grad_body(keep_ref, r1_ref, r2_ref, r3_ref, logit_ref, share_ref):
    total = four(keep_ref[...], r1_ref[...], r2_ref[...], r3_ref[...])
    logit_ref[...] = total[: logit_ref.shape[0], :].astype(BF16)
    for c in range(8):
        share_ref[c] = total[CLSP:, :].astype(BF16)


def z_sum_grad(keep, received, classes):
    return call(
        z_sum_grad_body,
        [((classes, BS), BF16), ((8, SHARE, BS), BF16)],
        (keep, *received),
    )


def aggregate_body(keep_ref, r1_ref, r2_ref, r3_ref, out_ref):
    out_ref[...] = four(keep_ref[...], r1_ref[...], r2_ref[...], r3_ref[...]).astype(BF16)


def aggregate(keep, received):
    return call(aggregate_body, [((BS, BS), BF16)], (keep, *received))[0]


def share_sum_body(parts_ref, out_ref):
    total = parts_ref[0].astype(F32)
    for c in range(1, 8):
        total = total + parts_ref[c].astype(F32)
    out_ref[...] = total


def share_sum(parts):
    return call(share_sum_body, [((SHARE, BS), F32)], (parts,))[0]


def unpack_body(me_ref, own_ref, r1_ref, r2_ref, r3_ref, in_ref, out_ref, all_ref):
    x = me_ref[0] // 8
    for d, ref in enumerate((own_ref, r1_ref, r2_ref, r3_ref)):
        all_ref[lax.bitwise_xor(d, x)] = ref[...]
    unit = 0
    for ref in (in_ref, out_ref):
        for side in range(2):
            for u in range(-(-ref.shape[0] // UNIT)):
                place, at = divmod(unit, UNITS)
                rows = min(UNIT, ref.shape[0] - u * UNIT)
                ref[u * UNIT : u * UNIT + rows, side * BS : (side + 1) * BS] = all_ref[
                    place, at * UNIT : at * UNIT + rows, :
                ]
                unit += 1


def unpack(me, own, received, classes):
    return call(
        unpack_body,
        [((128, 256), F32), ((classes, 256), F32)],
        (me, own, *received),
        [smem()] + [vmem()] * 4,
        [pltpu.VMEM((4, SHARE, BS), F32)],
    )


def permute(x, flip):
    return lax.ppermute(x, "row", [(i, i ^ flip) for i in range(32)])


def gather_col(x):
    far = lax.ppermute(x, "col", [(i, i ^ 4) for i in range(8)])
    pair = jnp.stack([x, far])
    return [pair] + [lax.ppermute(pair, "col", [(i, i ^ d) for i in range(8)]) for d in (1, 2, 3)]


CORE = 1
Z_FLIPS = (2, 4, 6)
X_FLIPS = (8, 16, 24)


def on_device(features, block_values, block_slots, block_counts, w_in, w_out, logit_grad):
    classes = logit_grad.shape[1]
    me = lax.axis_index("row").astype(jnp.int32).reshape(1)
    side = lax.axis_index("col").astype(jnp.int32).reshape(1)
    w_out_t = w_out.T
    parts = gather_col(features)
    grad_t = logit_grad.T
    cotangents = [grad_t] + [permute(grad_t, f) for f in Z_FLIPS]
    dense, grad_z = densify(me, side, block_counts, block_slots, block_values, cotangents)
    grad_x = [grad_z] + [permute(grad_z, f) for f in X_FLIPS]

    far = rows_product(dense, parts, 1, F32)
    got = permute(far, CORE)
    mine = rows_product(dense, parts, 0, F32)
    s1, s2, s3, keep, grad_near = core_sum(mine, got, grad_x)
    grad_far = permute(grad_near, CORE)
    s1, s2, s3, keep = x_sum(keep, [permute(s, f) for s, f in zip((s1, s2, s3), X_FLIPS)])
    received = [permute(s, f) for s, f in zip((s1, s2, s3), Z_FLIPS)]
    q = class_columns(grad_near, grad_far, dense)
    agg = gather_col(aggregate(keep, received))

    wide, far = class_rows_far(agg, w_in, w_out_t, q, me, dense)
    got = permute(far, CORE)
    mine = class_rows_near(wide, dense)
    s1, s2, s3, keep = core_sum_grad(mine, far, got)
    s1, s2, s3, keep = x_sum_grad(keep, [permute(s, f) for s, f in zip((s1, s2, s3), X_FLIPS)])
    received = [permute(s, f) for s, f in zip((s1, s2, s3), Z_FLIPS)]
    logits_t, shares = z_sum_grad(keep, received, classes)
    own = share_sum(lax.all_to_all(shares, "col", 0, 0))
    in_grad, out_grad_t = unpack(me, own, [permute(own, f) for f in X_FLIPS], classes)
    return (logits_t.T, in_grad, out_grad_t.T)


def solution(mesh):
    return jax.shard_map(
        on_device,
        mesh=mesh,
        in_specs=(
            P(("col", "row"), None),
            P(("row", "col"), None, None),
            P(("row", "col")),
            P(("row", "col")),
            P(),
            P(),
            P(("col", "row"), None),
        ),
        out_specs=(P(("col", "row"), None), P(), P()),
        check_vma=False,
    )
```

```python
import functools

import jax
import jax.numpy as jnp
from jax import lax
from jax.experimental import pallas as pl
from jax.experimental.pallas import tpu as pltpu
from jax.sharding import PartitionSpec as P

F32 = jnp.float32
BF16 = jnp.bfloat16
BS = 128
CLSP = 176
UNIT = 16
UNITS = 10
SHARE = UNITS * UNIT
VMEM_LIMIT = 32 * 1024 * 1024
STEP = 512
LOADS = 3
LOAD = 48


def vmem():
    return pl.BlockSpec(memory_space=pltpu.VMEM)


def smem():
    return pl.BlockSpec(memory_space=pltpu.SMEM)


def dot(a, b, da, db):
    return lax.dot_general(a, b, (((da,), (db,)), ((), ())), preferred_element_type=F32)


def call(body, outs, args, specs=None, scratch=(), flops=0):
    return pl.pallas_call(
        body,
        out_shape=[o if len(o) == 1 else jax.ShapeDtypeStruct(*o) for o in outs],
        in_specs=specs or [vmem()] * len(args),
        out_specs=[vmem()] * len(outs),
        scratch_shapes=scratch,
        compiler_params=pltpu.CompilerParams(vmem_limit_bytes=VMEM_LIMIT),
        cost_estimate=pl.CostEstimate(flops=flops, bytes_accessed=2**20, transcendentals=0),
    )(*args)


def hbm():
    return pl.BlockSpec(memory_space=pl.ANY)


def rows_of(dense_ref, first, i):
    at = (first + i) * STEP
    return dense_ref[at : at + STEP, :]


def densify_body(
    me_ref, side_ref, count_ref, slot_ref, block_ref, g0_ref, g1_ref, g2_ref, g3_ref,
    dense_ref, near_ref, held_ref, sem_ref,
):
    moves = [
        pltpu.make_async_copy(
            block_ref.at[pl.ds(i * LOAD, LOAD)], held_ref.at[pl.ds(i * LOAD, LOAD)], sem_ref.at[i]
        )
        for i in range(LOADS)
    ]
    for move in moves:
        move.start()
    dense_ref[...] = jnp.zeros_like(dense_ref)
    for d, ref in enumerate((g0_ref, g1_ref, g2_ref, g3_ref)):
        near_ref[d] = ref[...]
    me = me_ref[0]
    side = side_ref[0]
    count = count_ref[0]

    def place(b, carry):
        slot = slot_ref[b]
        rel = lax.bitwise_xor(slot // 8, me)
        at = (rel % 2) * 16 + rel // 2
        across = lax.bitwise_xor(slot % 8, side)
        row = pl.multiple_of(at * BS, BS)
        col = pl.multiple_of(((across % 4) * 2 + across // 4) * BS, BS)
        dense_ref[pl.ds(row, BS), pl.ds(col, BS)] = held_ref[b]
        return carry

    for i, move in enumerate(moves):
        move.wait()
        lax.fori_loop(i * LOAD, jnp.clip(count, i * LOAD, (i + 1) * LOAD), place, 0)


def densify(me, side, counts, slots, blocks, cotangents):
    return pl.pallas_call(
        densify_body,
        out_shape=[
            pltpu.VMEM((4096, 1024), BF16),
            jax.ShapeDtypeStruct((4,) + cotangents[0].shape, BF16),
        ],
        in_specs=[smem(), smem(), smem(), smem(), hbm()] + [vmem()] * 4,
        out_specs=[vmem(), vmem()],
        scratch_shapes=[pltpu.VMEM(blocks.shape, BF16), pltpu.SemaphoreType.DMA((LOADS,))],
        compiler_params=pltpu.CompilerParams(vmem_limit_bytes=52 * 1024 * 1024),
    )(me, side, counts, slots, blocks, *cotangents)


def joined(refs):
    return jnp.concatenate([ref[h] for ref in refs for h in range(2)])


def rows_product_body(half, dense_ref, r0_ref, r1_ref, r2_ref, r3_ref, out_ref):
    right = joined((r0_ref, r1_ref, r2_ref, r3_ref))
    for i in range(4):
        part = dot(rows_of(dense_ref, 4 * half, i), right, 1, 0)
        out_ref[i * STEP : (i + 1) * STEP, :] = part.astype(out_ref.dtype)


def rows_product(dense, parts, half, dtype):
    return call(
        functools.partial(rows_product_body, half),
        [((2048, BS), dtype)],
        (dense, *parts),
        [vmem()] * 5,
        flops=2 * 2048 * 1024 * 256,
    )[0]


def class_rows(wide, dense_ref, first, out_ref):
    for i in range(4):
        part = dot(wide, rows_of(dense_ref, first, i), 1, 1).astype(out_ref.dtype)
        for j in range(4):
            at = (i * 4 + j) * CLSP
            out_ref[at : at + CLSP, :] = part[:, j * BS : (j + 1) * BS]


def silu_inputs(agg, w_in_ref):
    pre = dot(agg, w_in_ref[...], 1, 0)
    gate = 1.0 / (1.0 + jnp.exp(-pre))
    return pre, gate, (pre * gate).astype(BF16)


def add_grads(pre, gate, hid, agg, q, w_out, x, out_ref):
    high = q.astype(BF16)
    low = (q - high.astype(F32)).astype(BF16)
    spread = dot(high, w_out, 0, 0) + dot(low, w_out, 0, 0)
    pre_grad = (spread * (gate * (1.0 + pre * (1.0 - gate)))).astype(BF16)
    in_grad = dot(agg, pre_grad, 0, 0)
    out_grad = dot(high, hid, 1, 0) + dot(low, hid, 1, 0)
    pieces = []
    for array in (in_grad, out_grad):
        rows = array.shape[0]
        over = -rows % UNIT
        if over:
            array = jnp.concatenate([array, jnp.zeros((over, array.shape[1]), F32)])
        array = array.astype(BF16)
        for side in range(2):
            pieces.append(array[:, side * BS : (side + 1) * BS])
    used = sum(piece.shape[0] for piece in pieces)
    pieces.append(jnp.zeros((4 * SHARE - used, BS), BF16))
    flat = jnp.concatenate(pieces)
    for j in range(4):
        at = pl.multiple_of(16 * CLSP + lax.bitwise_xor(j, x) * SHARE, UNIT)
        out_ref[pl.ds(at, SHARE), :] = flat[j * SHARE : (j + 1) * SHARE, :]


def class_rows_far_body(
    a0_ref, a1_ref, a2_ref, a3_ref, w_in_ref, w_out_ref, q_ref, me_ref, dense_ref,
    wide_ref, out_ref,
):
    agg = joined((a0_ref, a1_ref, a2_ref, a3_ref))
    pre, gate, hid = silu_inputs(agg, w_in_ref)
    wide = dot(w_out_ref[...], hid, 1, 1)
    zeros = jnp.zeros((CLSP - wide.shape[0], wide.shape[1]), F32)
    wide_ref[...] = jnp.concatenate([wide, zeros]).astype(BF16)
    class_rows(wide_ref[...], dense_ref, 4, out_ref)
    add_grads(pre, gate, hid, agg, q_ref[...], w_out_ref[...], me_ref[0] // 8, out_ref)


def class_rows_far(agg, w_in, w_out_t, q, me, dense):
    return call(
        class_rows_far_body,
        [((CLSP, 1024), BF16), ((16 * CLSP + 4 * SHARE, BS), BF16)],
        (*agg, w_in, w_out_t, q, me, dense),
        [vmem()] * 7 + [smem(), vmem()],
        flops=4 * 2048 * 1024 * 256,
    )


def class_rows_near_body(wide_ref, dense_ref, out_ref):
    class_rows(wide_ref[...], dense_ref, 0, out_ref)


def class_rows_near(wide, dense):
    return call(
        class_rows_near_body,
        [((16 * CLSP, BS), F32)],
        (wide, dense),
        flops=2 * 2048 * 1024 * 256,
    )[0]


def class_columns_body(near_ref, far_ref, dense_ref, out_ref):
    for i in range(8):
        ref = near_ref if i < 4 else far_ref
        left = jnp.concatenate([ref[(i % 4) * 4 + j] for j in range(4)], axis=1)
        part = dot(left, rows_of(dense_ref, 0, i), 1, 0)
        if i == 0:
            out_ref[...] = part
        else:
            out_ref[...] += part


def class_columns(near, far, dense):
    return call(
        class_columns_body,
        [((near.shape[1], 1024), F32)],
        (near, far, dense),
        flops=2 * 4096 * 1024 * 256,
    )[0]


def core_sum_body(mine_ref, got_ref, s1_ref, s2_ref, s3_ref, keep_ref):
    n = keep_ref.shape[0]
    for d, ref in ((1, s1_ref), (2, s2_ref), (3, s3_ref), (0, keep_ref)):
        at = slice(d * n, (d + 1) * n)
        ref[...] = (mine_ref[at, :] + got_ref[at, :]).astype(ref.dtype)


def core_sum(mine, got):
    shape = (mine.shape[0] // 4, BS)
    return call(core_sum_body, [(shape, BF16)] * 3 + [(shape, F32)], (mine, got))


def four(a, b, c, d):
    return (a.astype(F32) + b.astype(F32)) + (c.astype(F32) + d.astype(F32))


def x_sum_body(
    keep_ref, r1_ref, r2_ref, r3_ref, g0_ref, g1_ref, g2_ref, g3_ref,
    s1_ref, s2_ref, s3_ref, out_ref, grad_ref,
):
    n = out_ref.shape[0]
    for d, ref in ((1, s1_ref), (2, s2_ref), (3, s3_ref), (0, out_ref)):
        at = slice(d * n, (d + 1) * n)
        total = four(keep_ref[at, :], r1_ref[at, :], r2_ref[at, :], r3_ref[at, :])
        ref[...] = total.astype(ref.dtype)
    for d, ref in enumerate((g0_ref, g1_ref, g2_ref, g3_ref)):
        grad_ref[4 * d : 4 * d + 4] = ref[...]


def x_sum(keep, received, cotangents):
    shape = (keep.shape[0] // 4, BS)
    gathered = (16,) + cotangents[0].shape[1:]
    return call(
        x_sum_body,
        [(shape, BF16)] * 3 + [(shape, F32), (gathered, BF16)],
        (keep, *received, *cotangents),
    )


def core_sum_grad_body(mine_ref, far_ref, got_ref, s1_ref, s2_ref, s3_ref, keep_ref):
    n = 4 * CLSP
    for d, ref in ((1, s1_ref), (2, s2_ref), (3, s3_ref), (0, keep_ref)):
        at = slice(d * n, (d + 1) * n)
        ref[:n, :] = (mine_ref[at, :].astype(F32) + got_ref[at, :].astype(F32)).astype(ref.dtype)
        at = slice(4 * n + d * SHARE, 4 * n + (d + 1) * SHARE)
        ref[n:, :] = (far_ref[at, :].astype(F32) + got_ref[at, :].astype(F32)).astype(ref.dtype)


def core_sum_grad(mine, far, got):
    shape = (4 * CLSP + SHARE, BS)
    return call(core_sum_grad_body, [(shape, BF16)] * 3 + [(shape, F32)], (mine, far, got))


def x_sum_grad_body(keep_ref, r1_ref, r2_ref, r3_ref, s1_ref, s2_ref, s3_ref, out_ref):
    n = CLSP
    tail = slice(4 * n, 4 * n + SHARE)
    share = four(keep_ref[tail, :], r1_ref[tail, :], r2_ref[tail, :], r3_ref[tail, :])
    for d, ref in ((1, s1_ref), (2, s2_ref), (3, s3_ref), (0, out_ref)):
        at = slice(d * n, (d + 1) * n)
        total = four(keep_ref[at, :], r1_ref[at, :], r2_ref[at, :], r3_ref[at, :])
        ref[:n, :] = total.astype(ref.dtype)
        ref[n:, :] = share.astype(BF16).astype(ref.dtype)


def x_sum_grad(keep, received):
    shape = (CLSP + SHARE, BS)
    return call(x_sum_grad_body, [(shape, BF16)] * 3 + [(shape, F32)], (keep, *received))


def z_sum_grad_body(keep_ref, r1_ref, r2_ref, r3_ref, logit_ref, share_ref):
    total = four(keep_ref[...], r1_ref[...], r2_ref[...], r3_ref[...])
    logit_ref[...] = total[: logit_ref.shape[0], :].astype(BF16)
    for c in range(8):
        share_ref[c] = total[CLSP:, :].astype(BF16)


def z_sum_grad(keep, received, classes):
    return call(
        z_sum_grad_body,
        [((classes, BS), BF16), ((8, SHARE, BS), BF16)],
        (keep, *received),
    )


def aggregate_body(keep_ref, r1_ref, r2_ref, r3_ref, out_ref):
    out_ref[...] = four(keep_ref[...], r1_ref[...], r2_ref[...], r3_ref[...]).astype(BF16)


def aggregate(keep, received):
    return call(aggregate_body, [((BS, BS), BF16)], (keep, *received))[0]


def share_sum_body(parts_ref, out_ref):
    total = parts_ref[0].astype(F32)
    for c in range(1, 8):
        total = total + parts_ref[c].astype(F32)
    out_ref[...] = total


def share_sum(parts):
    return call(share_sum_body, [((SHARE, BS), F32)], (parts,))[0]


def unpack_body(me_ref, own_ref, r1_ref, r2_ref, r3_ref, in_ref, out_ref, all_ref):
    x = me_ref[0] // 8
    for d, ref in enumerate((own_ref, r1_ref, r2_ref, r3_ref)):
        all_ref[lax.bitwise_xor(d, x)] = ref[...]
    unit = 0
    for ref in (in_ref, out_ref):
        for side in range(2):
            for u in range(-(-ref.shape[0] // UNIT)):
                place, at = divmod(unit, UNITS)
                rows = min(UNIT, ref.shape[0] - u * UNIT)
                ref[u * UNIT : u * UNIT + rows, side * BS : (side + 1) * BS] = all_ref[
                    place, at * UNIT : at * UNIT + rows, :
                ]
                unit += 1


def unpack(me, own, received, classes):
    return call(
        unpack_body,
        [((128, 256), F32), ((classes, 256), F32)],
        (me, own, *received),
        [smem()] + [vmem()] * 4,
        [pltpu.VMEM((4, SHARE, BS), F32)],
    )


def permute(x, flip):
    return lax.ppermute(x, "row", [(i, i ^ flip) for i in range(32)])


def gather_col(x):
    far = lax.ppermute(x, "col", [(i, i ^ 4) for i in range(8)])
    pair = jnp.stack([x, far])
    return [pair] + [lax.ppermute(pair, "col", [(i, i ^ d) for i in range(8)]) for d in (1, 2, 3)]


CORE = 1
Z_FLIPS = (2, 4, 6)
X_FLIPS = (8, 16, 24)


def on_device(features, block_values, block_slots, block_counts, w_in, w_out, logit_grad):
    classes = logit_grad.shape[1]
    me = lax.axis_index("row").astype(jnp.int32).reshape(1)
    side = lax.axis_index("col").astype(jnp.int32).reshape(1)
    w_out_t = w_out.T
    parts = gather_col(features)
    grad_t = logit_grad.T
    cotangents = [grad_t] + [permute(grad_t, f) for f in Z_FLIPS]
    dense, grad_z = densify(me, side, block_counts, block_slots, block_values, cotangents)
    far = rows_product(dense, parts, 1, F32)
    got = permute(far, CORE)
    mine = rows_product(dense, parts, 0, F32)
    s1, s2, s3, keep = core_sum(mine, got)
    received = [permute(s, f) for s, f in zip((s1, s2, s3), X_FLIPS)]
    grad_x = [grad_z] + [permute(grad_z, f) for f in X_FLIPS]
    s1, s2, s3, keep, grad_near = x_sum(keep, received, grad_x)
    grad_far = permute(grad_near, CORE)
    received = [permute(s, f) for s, f in zip((s1, s2, s3), Z_FLIPS)]
    q = class_columns(grad_near, grad_far, dense)
    agg = gather_col(aggregate(keep, received))

    wide, far = class_rows_far(agg, w_in, w_out_t, q, me, dense)
    got = permute(far, CORE)
    mine = class_rows_near(wide, dense)
    s1, s2, s3, keep = core_sum_grad(mine, far, got)
    s1, s2, s3, keep = x_sum_grad(keep, [permute(s, f) for s, f in zip((s1, s2, s3), X_FLIPS)])
    received = [permute(s, f) for s, f in zip((s1, s2, s3), Z_FLIPS)]
    logits_t, shares = z_sum_grad(keep, received, classes)
    own = share_sum(lax.all_to_all(shares, "col", 0, 0))
    in_grad, out_grad_t = unpack(me, own, [permute(own, f) for f in X_FLIPS], classes)
    return (logits_t.T, in_grad, out_grad_t.T)


def solution(mesh):
    return jax.shard_map(
        on_device,
        mesh=mesh,
        in_specs=(
            P(("col", "row"), None),
            P(("row", "col"), None, None),
            P(("row", "col")),
            P(("row", "col")),
            P(),
            P(),
            P(("col", "row"), None),
        ),
        out_specs=(P(("col", "row"), None), P(), P()),
        check_vma=False,
    )
```

```python
import jax
import jax.numpy as jnp
from jax import lax
from jax.experimental import pallas as pl
from jax.experimental.pallas import tpu as pltpu
from jax.sharding import PartitionSpec as P

F32 = jnp.float32
BF16 = jnp.bfloat16
BS = 128
CLSP = 176
UNIT = 16
UNITS = 10
SHARE = UNITS * UNIT
VMEM_LIMIT = 32 * 1024 * 1024
STEP = 512
LOADS = 3
LOAD = 48


def vmem():
    return pl.BlockSpec(memory_space=pltpu.VMEM)


def smem():
    return pl.BlockSpec(memory_space=pltpu.SMEM)


def dot(a, b, da, db):
    return lax.dot_general(a, b, (((da,), (db,)), ((), ())), preferred_element_type=F32)


def call(body, outs, args, specs=None, scratch=(), flops=0):
    return pl.pallas_call(
        body,
        out_shape=[o if len(o) == 1 else jax.ShapeDtypeStruct(*o) for o in outs],
        in_specs=specs or [vmem()] * len(args),
        out_specs=[vmem()] * len(outs),
        scratch_shapes=scratch,
        compiler_params=pltpu.CompilerParams(vmem_limit_bytes=VMEM_LIMIT),
        cost_estimate=pl.CostEstimate(flops=flops, bytes_accessed=2**20, transcendentals=0),
    )(*args)


def hbm():
    return pl.BlockSpec(memory_space=pl.ANY)


def rows_of(dense_ref, first, i):
    at = (first + i) * STEP
    return dense_ref[at : at + STEP, :]


def densify_body(
    me_ref, side_ref, count_ref, slot_ref, block_ref, dense_ref, held_ref, sem_ref
):
    moves = [
        pltpu.make_async_copy(
            block_ref.at[pl.ds(i * LOAD, LOAD)], held_ref.at[pl.ds(i * LOAD, LOAD)], sem_ref.at[i]
        )
        for i in range(LOADS)
    ]
    for move in moves:
        move.start()
    dense_ref[...] = jnp.zeros_like(dense_ref)
    me = me_ref[0]
    side = side_ref[0]
    count = count_ref[0]

    def place(b, carry):
        slot = slot_ref[b]
        rel = lax.bitwise_xor(slot // 8, me)
        at = (rel % 2) * 16 + rel // 2
        across = lax.bitwise_xor(slot % 8, side)
        row = pl.multiple_of(at * BS, BS)
        col = pl.multiple_of(((across % 4) * 2 + across // 4) * BS, BS)
        dense_ref[pl.ds(row, BS), pl.ds(col, BS)] = held_ref[b]
        return carry

    for i, move in enumerate(moves):
        move.wait()
        lax.fori_loop(i * LOAD, jnp.clip(count, i * LOAD, (i + 1) * LOAD), place, 0)


def densify(me, side, counts, slots, blocks):
    return pl.pallas_call(
        densify_body,
        out_shape=pltpu.VMEM((4096, 1024), BF16),
        in_specs=[smem(), smem(), smem(), smem(), hbm()],
        out_specs=vmem(),
        scratch_shapes=[pltpu.VMEM(blocks.shape, BF16), pltpu.SemaphoreType.DMA((LOADS,))],
        compiler_params=pltpu.CompilerParams(vmem_limit_bytes=52 * 1024 * 1024),
    )(me, side, counts, slots, blocks)


def joined(refs):
    return jnp.concatenate([ref[h] for ref in refs for h in range(2)])


def rows_product_step(half, dense_ref, right_refs, out_ref):
    right = joined(right_refs)
    for i in range(4):
        out_ref[i * STEP : (i + 1) * STEP, :] = dot(rows_of(dense_ref, 4 * half, i), right, 1, 0)


def rows_product_far_body(
    dense_ref, r0_ref, r1_ref, r2_ref, r3_ref, g0_ref, g1_ref, g2_ref, g3_ref, out_ref, grad_ref
):
    for d, ref in enumerate((g0_ref, g1_ref, g2_ref, g3_ref)):
        grad_ref[d] = ref[...]
    rows_product_step(1, dense_ref, (r0_ref, r1_ref, r2_ref, r3_ref), out_ref)


def rows_product_far(dense, parts, cotangents):
    return call(
        rows_product_far_body,
        [((2048, BS), F32), ((4,) + cotangents[0].shape, BF16)],
        (dense, *parts, *cotangents),
        flops=2 * 2048 * 1024 * 256,
    )


def rows_product_near_body(dense_ref, r0_ref, r1_ref, r2_ref, r3_ref, out_ref):
    rows_product_step(0, dense_ref, (r0_ref, r1_ref, r2_ref, r3_ref), out_ref)


def rows_product_near(dense, parts):
    return call(
        rows_product_near_body,
        [((2048, BS), F32)],
        (dense, *parts),
        flops=2 * 2048 * 1024 * 256,
    )[0]


def class_rows(wide, dense_ref, first, out_ref):
    for i in range(4):
        part = dot(wide, rows_of(dense_ref, first, i), 1, 1).astype(out_ref.dtype)
        for j in range(4):
            at = (i * 4 + j) * CLSP
            out_ref[at : at + CLSP, :] = part[:, j * BS : (j + 1) * BS]


def silu_inputs(agg, w_in_ref):
    pre = dot(agg, w_in_ref[...], 1, 0)
    gate = 1.0 / (1.0 + jnp.exp(-pre))
    return pre, gate, (pre * gate).astype(BF16)


def add_grads(pre, gate, hid, agg, q, w_out, x, out_ref):
    high = q.astype(BF16)
    low = (q - high.astype(F32)).astype(BF16)
    spread = dot(high, w_out, 0, 0) + dot(low, w_out, 0, 0)
    pre_grad = spread * (gate * (1.0 + pre * (1.0 - gate)))
    pre_high = pre_grad.astype(BF16)
    pre_low = (pre_grad - pre_high.astype(F32)).astype(BF16)
    in_grad = dot(agg, pre_high, 0, 0) + dot(agg, pre_low, 0, 0)
    out_grad = dot(high, hid, 1, 0) + dot(low, hid, 1, 0)
    pieces = []
    for array in (in_grad, out_grad):
        rows = array.shape[0]
        over = -rows % UNIT
        if over:
            array = jnp.concatenate([array, jnp.zeros((over, array.shape[1]), F32)])
        array = array.astype(BF16)
        for side in range(2):
            pieces.append(array[:, side * BS : (side + 1) * BS])
    used = sum(piece.shape[0] for piece in pieces)
    pieces.append(jnp.zeros((4 * SHARE - used, BS), BF16))
    flat = jnp.concatenate(pieces)
    for j in range(4):
        at = pl.multiple_of(16 * CLSP + lax.bitwise_xor(j, x) * SHARE, UNIT)
        out_ref[pl.ds(at, SHARE), :] = flat[j * SHARE : (j + 1) * SHARE, :]


def class_rows_far_body(
    a0_ref, a1_ref, a2_ref, a3_ref, w_in_ref, w_out_ref, q_ref, me_ref, dense_ref,
    wide_ref, out_ref,
):
    agg = joined((a0_ref, a1_ref, a2_ref, a3_ref))
    pre, gate, hid = silu_inputs(agg, w_in_ref)
    wide = dot(w_out_ref[...], hid, 1, 1)
    zeros = jnp.zeros((CLSP - wide.shape[0], wide.shape[1]), F32)
    wide_ref[...] = jnp.concatenate([wide, zeros]).astype(BF16)
    class_rows(wide_ref[...], dense_ref, 4, out_ref)
    add_grads(pre, gate, hid, agg, q_ref[...], w_out_ref[...], me_ref[0] // 8, out_ref)


def class_rows_far(agg, w_in, w_out_t, q, me, dense):
    return call(
        class_rows_far_body,
        [((CLSP, 1024), BF16), ((16 * CLSP + 4 * SHARE, BS), BF16)],
        (*agg, w_in, w_out_t, q, me, dense),
        [vmem()] * 7 + [smem(), vmem()],
        flops=4 * 2048 * 1024 * 256,
    )


def class_rows_near_body(wide_ref, dense_ref, out_ref):
    class_rows(wide_ref[...], dense_ref, 0, out_ref)


def class_rows_near(wide, dense):
    return call(
        class_rows_near_body,
        [((16 * CLSP, BS), F32)],
        (wide, dense),
        flops=2 * 2048 * 1024 * 256,
    )[0]


def class_columns_body(near_ref, far_ref, dense_ref, out_ref):
    for i in range(8):
        ref = near_ref if i < 4 else far_ref
        left = jnp.concatenate([ref[(i % 4) * 4 + j] for j in range(4)], axis=1)
        part = dot(left, rows_of(dense_ref, 0, i), 1, 0)
        if i == 0:
            out_ref[...] = part
        else:
            out_ref[...] += part


def class_columns(near, far, dense):
    return call(
        class_columns_body,
        [((near.shape[1], 1024), F32)],
        (near, far, dense),
        flops=2 * 4096 * 1024 * 256,
    )[0]


def core_sum_body(mine_ref, got_ref, s1_ref, s2_ref, s3_ref, keep_ref):
    n = keep_ref.shape[0]
    for d, ref in ((1, s1_ref), (2, s2_ref), (3, s3_ref), (0, keep_ref)):
        at = slice(d * n, (d + 1) * n)
        ref[...] = (mine_ref[at, :] + got_ref[at, :]).astype(ref.dtype)


def core_sum(mine, got):
    shape = (mine.shape[0] // 4, BS)
    return call(core_sum_body, [(shape, BF16)] * 3 + [(shape, F32)], (mine, got))


def four(a, b, c, d):
    return (a.astype(F32) + b.astype(F32)) + (c.astype(F32) + d.astype(F32))


def x_sum_body(
    keep_ref, r1_ref, r2_ref, r3_ref, g0_ref, g1_ref, g2_ref, g3_ref,
    s1_ref, s2_ref, s3_ref, out_ref, grad_ref,
):
    n = out_ref.shape[0]
    for d, ref in ((1, s1_ref), (2, s2_ref), (3, s3_ref), (0, out_ref)):
        at = slice(d * n, (d + 1) * n)
        total = four(keep_ref[at, :], r1_ref[at, :], r2_ref[at, :], r3_ref[at, :])
        ref[...] = total.astype(ref.dtype)
    for d, ref in enumerate((g0_ref, g1_ref, g2_ref, g3_ref)):
        grad_ref[4 * d : 4 * d + 4] = ref[...]


def x_sum(keep, received, cotangents):
    shape = (keep.shape[0] // 4, BS)
    gathered = (16,) + cotangents[0].shape[1:]
    return call(
        x_sum_body,
        [(shape, BF16)] * 3 + [(shape, F32), (gathered, BF16)],
        (keep, *received, *cotangents),
    )


def core_sum_grad_body(mine_ref, far_ref, got_ref, s1_ref, s2_ref, s3_ref, keep_ref):
    n = 4 * CLSP
    for d, ref in ((1, s1_ref), (2, s2_ref), (3, s3_ref), (0, keep_ref)):
        at = slice(d * n, (d + 1) * n)
        ref[:n, :] = (mine_ref[at, :].astype(F32) + got_ref[at, :].astype(F32)).astype(ref.dtype)
        at = slice(4 * n + d * SHARE, 4 * n + (d + 1) * SHARE)
        ref[n:, :] = (far_ref[at, :].astype(F32) + got_ref[at, :].astype(F32)).astype(ref.dtype)


def core_sum_grad(mine, far, got):
    shape = (4 * CLSP + SHARE, BS)
    return call(core_sum_grad_body, [(shape, BF16)] * 3 + [(shape, F32)], (mine, far, got))


def x_sum_grad_body(keep_ref, r1_ref, r2_ref, r3_ref, s1_ref, s2_ref, s3_ref, out_ref):
    n = CLSP
    tail = slice(4 * n, 4 * n + SHARE)
    share = four(keep_ref[tail, :], r1_ref[tail, :], r2_ref[tail, :], r3_ref[tail, :])
    for d, ref in ((1, s1_ref), (2, s2_ref), (3, s3_ref), (0, out_ref)):
        at = slice(d * n, (d + 1) * n)
        total = four(keep_ref[at, :], r1_ref[at, :], r2_ref[at, :], r3_ref[at, :])
        ref[:n, :] = total.astype(ref.dtype)
        ref[n:, :] = share.astype(BF16).astype(ref.dtype)


def x_sum_grad(keep, received):
    shape = (CLSP + SHARE, BS)
    return call(x_sum_grad_body, [(shape, BF16)] * 3 + [(shape, F32)], (keep, *received))


def z_sum_grad_body(keep_ref, r1_ref, r2_ref, r3_ref, logit_ref, share_ref):
    total = four(keep_ref[...], r1_ref[...], r2_ref[...], r3_ref[...])
    logit_ref[...] = total[: logit_ref.shape[0], :].astype(BF16)
    for c in range(8):
        share_ref[c] = total[CLSP:, :].astype(BF16)


def z_sum_grad(keep, received, classes):
    return call(
        z_sum_grad_body,
        [((classes, BS), BF16), ((8, SHARE, BS), BF16)],
        (keep, *received),
    )


def aggregate_body(keep_ref, r1_ref, r2_ref, r3_ref, out_ref):
    out_ref[...] = four(keep_ref[...], r1_ref[...], r2_ref[...], r3_ref[...]).astype(BF16)


def aggregate(keep, received):
    return call(aggregate_body, [((BS, BS), BF16)], (keep, *received))[0]


def share_sum_body(parts_ref, out_ref):
    total = parts_ref[0].astype(F32)
    for c in range(1, 8):
        total = total + parts_ref[c].astype(F32)
    out_ref[...] = total


def share_sum(parts):
    return call(share_sum_body, [((SHARE, BS), F32)], (parts,))[0]


def unpack_body(me_ref, own_ref, r1_ref, r2_ref, r3_ref, in_ref, out_ref, all_ref):
    x = me_ref[0] // 8
    for d, ref in enumerate((own_ref, r1_ref, r2_ref, r3_ref)):
        all_ref[lax.bitwise_xor(d, x)] = ref[...]
    unit = 0
    for ref in (in_ref, out_ref):
        for side in range(2):
            for u in range(-(-ref.shape[0] // UNIT)):
                place, at = divmod(unit, UNITS)
                rows = min(UNIT, ref.shape[0] - u * UNIT)
                ref[u * UNIT : u * UNIT + rows, side * BS : (side + 1) * BS] = all_ref[
                    place, at * UNIT : at * UNIT + rows, :
                ]
                unit += 1


def unpack(me, own, received, classes):
    return call(
        unpack_body,
        [((128, 256), F32), ((classes, 256), F32)],
        (me, own, *received),
        [smem()] + [vmem()] * 4,
        [pltpu.VMEM((4, SHARE, BS), F32)],
    )


def permute(x, flip):
    return lax.ppermute(x, "row", [(i, i ^ flip) for i in range(32)])


def gather_col(x):
    far = lax.ppermute(x, "col", [(i, i ^ 4) for i in range(8)])
    pair = jnp.stack([x, far])
    return [pair] + [lax.ppermute(pair, "col", [(i, i ^ d) for i in range(8)]) for d in (1, 2, 3)]


CORE = 1
Z_FLIPS = (2, 4, 6)
X_FLIPS = (8, 16, 24)


def on_device(features, block_values, block_slots, block_counts, w_in, w_out, logit_grad):
    classes = logit_grad.shape[1]
    me = lax.axis_index("row").astype(jnp.int32).reshape(1)
    side = lax.axis_index("col").astype(jnp.int32).reshape(1)
    w_out_t = w_out.T
    parts = gather_col(features)
    grad_t = logit_grad.T
    cotangents = [grad_t] + [permute(grad_t, f) for f in Z_FLIPS]
    dense = densify(me, side, block_counts, block_slots, block_values)
    far, grad_z = rows_product_far(dense, parts, cotangents)
    got = permute(far, CORE)
    mine = rows_product_near(dense, parts)
    s1, s2, s3, keep = core_sum(mine, got)
    received = [permute(s, f) for s, f in zip((s1, s2, s3), X_FLIPS)]
    grad_x = [grad_z] + [permute(grad_z, f) for f in X_FLIPS]
    s1, s2, s3, keep, grad_near = x_sum(keep, received, grad_x)
    grad_far = permute(grad_near, CORE)
    received = [permute(s, f) for s, f in zip((s1, s2, s3), Z_FLIPS)]
    q = class_columns(grad_near, grad_far, dense)
    agg = gather_col(aggregate(keep, received))

    wide, far = class_rows_far(agg, w_in, w_out_t, q, me, dense)
    got = permute(far, CORE)
    mine = class_rows_near(wide, dense)
    s1, s2, s3, keep = core_sum_grad(mine, far, got)
    s1, s2, s3, keep = x_sum_grad(keep, [permute(s, f) for s, f in zip((s1, s2, s3), X_FLIPS)])
    received = [permute(s, f) for s, f in zip((s1, s2, s3), Z_FLIPS)]
    logits_t, shares = z_sum_grad(keep, received, classes)
    own = share_sum(lax.all_to_all(shares, "col", 0, 0))
    in_grad, out_grad_t = unpack(me, own, [permute(own, f) for f in X_FLIPS], classes)
    return (logits_t.T, in_grad, out_grad_t.T)


def solution(mesh):
    return jax.shard_map(
        on_device,
        mesh=mesh,
        in_specs=(
            P(("col", "row"), None),
            P(("row", "col"), None, None),
            P(("row", "col")),
            P(("row", "col")),
            P(),
            P(),
            P(("col", "row"), None),
        ),
        out_specs=(P(("col", "row"), None), P(), P()),
        check_vma=False,
    )
```

```python
import jax
import jax.numpy as jnp
from jax import lax
from jax.experimental import pallas as pl
from jax.experimental.pallas import tpu as pltpu
from jax.sharding import PartitionSpec as P

F32 = jnp.float32
BF16 = jnp.bfloat16
BS = 128
CLSP = 176
UNIT = 16
UNITS = 10
SHARE = UNITS * UNIT
VMEM_LIMIT = 32 * 1024 * 1024
STEP = 512
LOADS = 3
LOAD = 48


def vmem():
    return pl.BlockSpec(memory_space=pltpu.VMEM)


def smem():
    return pl.BlockSpec(memory_space=pltpu.SMEM)


def dot(a, b, da, db):
    return lax.dot_general(a, b, (((da,), (db,)), ((), ())), preferred_element_type=F32)


def call(body, outs, args, specs=None, scratch=(), flops=0):
    return pl.pallas_call(
        body,
        out_shape=[o if len(o) == 1 else jax.ShapeDtypeStruct(*o) for o in outs],
        in_specs=specs or [vmem()] * len(args),
        out_specs=[vmem()] * len(outs),
        scratch_shapes=scratch,
        compiler_params=pltpu.CompilerParams(vmem_limit_bytes=VMEM_LIMIT),
        cost_estimate=pl.CostEstimate(flops=flops, bytes_accessed=2**20, transcendentals=0),
    )(*args)


def hbm():
    return pl.BlockSpec(memory_space=pl.ANY)


def rows_of(dense_ref, first, i):
    at = (first + i) * STEP
    return dense_ref[at : at + STEP, :]


def densify_body(
    me_ref, side_ref, count_ref, slot_ref, block_ref, dense_ref, held_ref, sem_ref
):
    moves = [
        pltpu.make_async_copy(
            block_ref.at[pl.ds(i * LOAD, LOAD)], held_ref.at[pl.ds(i * LOAD, LOAD)], sem_ref.at[i]
        )
        for i in range(LOADS)
    ]
    for move in moves:
        move.start()
    dense_ref[...] = jnp.zeros_like(dense_ref)
    me = me_ref[0]
    side = side_ref[0]
    count = count_ref[0]

    def place(b, carry):
        slot = slot_ref[b]
        rel = lax.bitwise_xor(slot // 8, me)
        at = (rel % 2) * 16 + rel // 2
        across = lax.bitwise_xor(slot % 8, side)
        row = pl.multiple_of(at * BS, BS)
        col = pl.multiple_of(((across % 4) * 2 + across // 4) * BS, BS)
        dense_ref[pl.ds(row, BS), pl.ds(col, BS)] = held_ref[b]
        return carry

    for i, move in enumerate(moves):
        move.wait()
        lax.fori_loop(i * LOAD, jnp.clip(count, i * LOAD, (i + 1) * LOAD), place, 0)


def densify(me, side, counts, slots, blocks):
    return pl.pallas_call(
        densify_body,
        out_shape=pltpu.VMEM((4096, 1024), BF16),
        in_specs=[smem(), smem(), smem(), smem(), hbm()],
        out_specs=vmem(),
        scratch_shapes=[pltpu.VMEM(blocks.shape, BF16), pltpu.SemaphoreType.DMA((LOADS,))],
        compiler_params=pltpu.CompilerParams(vmem_limit_bytes=52 * 1024 * 1024),
    )(me, side, counts, slots, blocks)


def joined(refs):
    return jnp.concatenate([ref[h] for ref in refs for h in range(2)])


def rows_product_step(half, dense_ref, right_refs, out_ref):
    right = joined(right_refs)
    for i in range(4):
        out_ref[i * STEP : (i + 1) * STEP, :] = dot(rows_of(dense_ref, 4 * half, i), right, 1, 0)


def rows_product_far_body(
    dense_ref, r0_ref, r1_ref, r2_ref, r3_ref, g0_ref, g1_ref, g2_ref, g3_ref, out_ref, grad_ref
):
    for d, ref in enumerate((g0_ref, g1_ref, g2_ref, g3_ref)):
        grad_ref[d] = ref[...]
    rows_product_step(1, dense_ref, (r0_ref, r1_ref, r2_ref, r3_ref), out_ref)


def rows_product_far(dense, parts, cotangents):
    return call(
        rows_product_far_body,
        [((2048, BS), F32), ((4,) + cotangents[0].shape, BF16)],
        (dense, *parts, *cotangents),
        flops=2 * 2048 * 1024 * 256,
    )


def rows_product_near_body(dense_ref, r0_ref, r1_ref, r2_ref, r3_ref, out_ref):
    rows_product_step(0, dense_ref, (r0_ref, r1_ref, r2_ref, r3_ref), out_ref)


def rows_product_near(dense, parts):
    return call(
        rows_product_near_body,
        [((2048, BS), F32)],
        (dense, *parts),
        flops=2 * 2048 * 1024 * 256,
    )[0]


def class_rows(wide, dense_ref, first, out_ref):
    for i in range(4):
        part = dot(wide, rows_of(dense_ref, first, i), 1, 1).astype(out_ref.dtype)
        for j in range(4):
            at = (i * 4 + j) * CLSP
            out_ref[at : at + CLSP, :] = part[:, j * BS : (j + 1) * BS]


def silu_inputs(agg, w_in_ref):
    pre = dot(agg, w_in_ref[...], 1, 0)
    gate = 1.0 / (1.0 + jnp.exp(-pre))
    return pre, gate, (pre * gate).astype(BF16)


def add_grads(pre, gate, hid, agg, q, w_out, x, out_ref):
    high = q.astype(BF16)
    low = (q - high.astype(F32)).astype(BF16)
    spread = dot(high, w_out, 0, 0) + dot(low, w_out, 0, 0)
    pre_grad = spread * (gate * (1.0 + pre * (1.0 - gate)))
    pre_high = pre_grad.astype(BF16)
    pre_low = (pre_grad - pre_high.astype(F32)).astype(BF16)
    in_grad = dot(agg, pre_high, 0, 0) + dot(agg, pre_low, 0, 0)
    out_grad = dot(high, hid, 1, 0) + dot(low, hid, 1, 0)
    pieces = []
    for array in (in_grad, out_grad):
        rows = array.shape[0]
        over = -rows % UNIT
        if over:
            array = jnp.concatenate([array, jnp.zeros((over, array.shape[1]), F32)])
        array = array.astype(BF16)
        for side in range(2):
            pieces.append(array[:, side * BS : (side + 1) * BS])
    used = sum(piece.shape[0] for piece in pieces)
    pieces.append(jnp.zeros((4 * SHARE - used, BS), BF16))
    flat = jnp.concatenate(pieces)
    for j in range(4):
        at = pl.multiple_of(16 * CLSP + lax.bitwise_xor(j, x) * SHARE, UNIT)
        out_ref[pl.ds(at, SHARE), :] = flat[j * SHARE : (j + 1) * SHARE, :]


def class_rows_far_body(
    a0_ref, a1_ref, a2_ref, a3_ref, w_in_ref, w_out_ref, q_ref, me_ref, dense_ref,
    wide_ref, out_ref,
):
    agg = joined((a0_ref, a1_ref, a2_ref, a3_ref))
    pre, gate, hid = silu_inputs(agg, w_in_ref)
    wide = dot(w_out_ref[...], hid, 1, 1)
    zeros = jnp.zeros((CLSP - wide.shape[0], wide.shape[1]), F32)
    wide_ref[...] = jnp.concatenate([wide, zeros]).astype(BF16)
    class_rows(wide_ref[...], dense_ref, 4, out_ref)
    add_grads(pre, gate, hid, agg, q_ref[...], w_out_ref[...], me_ref[0] // 8, out_ref)


def class_rows_far(agg, w_in, w_out_t, q, me, dense):
    return call(
        class_rows_far_body,
        [((CLSP, 1024), BF16), ((16 * CLSP + 4 * SHARE, BS), BF16)],
        (*agg, w_in, w_out_t, q, me, dense),
        [vmem()] * 7 + [smem(), vmem()],
        flops=4 * 2048 * 1024 * 256,
    )


def class_rows_near_body(wide_ref, dense_ref, out_ref):
    class_rows(wide_ref[...], dense_ref, 0, out_ref)


def class_rows_near(wide, dense):
    return call(
        class_rows_near_body,
        [((16 * CLSP, BS), F32)],
        (wide, dense),
        flops=2 * 2048 * 1024 * 256,
    )[0]


def class_columns_body(near_ref, far_ref, dense_ref, out_ref):
    for i in range(8):
        ref = near_ref if i < 4 else far_ref
        left = jnp.concatenate([ref[(i % 4) * 4 + j] for j in range(4)], axis=1)
        part = dot(left, rows_of(dense_ref, 0, i), 1, 0)
        if i == 0:
            out_ref[...] = part
        else:
            out_ref[...] += part


def class_columns(near, far, dense):
    return call(
        class_columns_body,
        [((near.shape[1], 1024), F32)],
        (near, far, dense),
        flops=2 * 4096 * 1024 * 256,
    )[0]


def core_sum_body(mine_ref, got_ref, s1_ref, s2_ref, s3_ref, keep_ref):
    n = keep_ref.shape[0]
    for d, ref in ((1, s1_ref), (2, s2_ref), (3, s3_ref), (0, keep_ref)):
        at = slice(d * n, (d + 1) * n)
        ref[...] = (mine_ref[at, :] + got_ref[at, :]).astype(ref.dtype)


def core_sum(mine, got):
    shape = (mine.shape[0] // 4, BS)
    return call(core_sum_body, [(shape, BF16)] * 3 + [(shape, F32)], (mine, got))


def four(a, b, c, d):
    return (a.astype(F32) + b.astype(F32)) + (c.astype(F32) + d.astype(F32))


def x_sum_body(keep_ref, r1_ref, r2_ref, r3_ref, s1_ref, s2_ref, s3_ref, out_ref):
    n = out_ref.shape[0]
    for d, ref in ((1, s1_ref), (2, s2_ref), (3, s3_ref), (0, out_ref)):
        at = slice(d * n, (d + 1) * n)
        total = four(keep_ref[at, :], r1_ref[at, :], r2_ref[at, :], r3_ref[at, :])
        ref[...] = total.astype(ref.dtype)


def x_sum(keep, received):
    shape = (keep.shape[0] // 4, BS)
    return call(x_sum_body, [(shape, BF16)] * 3 + [(shape, F32)], (keep, *received))


def core_sum_grad_body(mine_ref, far_ref, got_ref, s1_ref, s2_ref, s3_ref, keep_ref):
    n = 4 * CLSP
    for d, ref in ((1, s1_ref), (2, s2_ref), (3, s3_ref), (0, keep_ref)):
        at = slice(d * n, (d + 1) * n)
        ref[:n, :] = (mine_ref[at, :].astype(F32) + got_ref[at, :].astype(F32)).astype(ref.dtype)
        at = slice(4 * n + d * SHARE, 4 * n + (d + 1) * SHARE)
        ref[n:, :] = (far_ref[at, :].astype(F32) + got_ref[at, :].astype(F32)).astype(ref.dtype)


def core_sum_grad(mine, far, got):
    shape = (4 * CLSP + SHARE, BS)
    return call(core_sum_grad_body, [(shape, BF16)] * 3 + [(shape, F32)], (mine, far, got))


def x_sum_grad_body(keep_ref, r1_ref, r2_ref, r3_ref, s1_ref, s2_ref, s3_ref, out_ref):
    n = CLSP
    tail = slice(4 * n, 4 * n + SHARE)
    share = four(keep_ref[tail, :], r1_ref[tail, :], r2_ref[tail, :], r3_ref[tail, :])
    for d, ref in ((1, s1_ref), (2, s2_ref), (3, s3_ref), (0, out_ref)):
        at = slice(d * n, (d + 1) * n)
        total = four(keep_ref[at, :], r1_ref[at, :], r2_ref[at, :], r3_ref[at, :])
        ref[:n, :] = total.astype(ref.dtype)
        ref[n:, :] = share.astype(BF16).astype(ref.dtype)


def x_sum_grad(keep, received):
    shape = (CLSP + SHARE, BS)
    return call(x_sum_grad_body, [(shape, BF16)] * 3 + [(shape, F32)], (keep, *received))


def z_sum_grad_body(keep_ref, r1_ref, r2_ref, r3_ref, logit_ref, share_ref):
    total = four(keep_ref[...], r1_ref[...], r2_ref[...], r3_ref[...])
    logit_ref[...] = total[: logit_ref.shape[0], :].astype(BF16)
    for c in range(8):
        share_ref[c] = total[CLSP:, :].astype(BF16)


def z_sum_grad(keep, received, classes):
    return call(
        z_sum_grad_body,
        [((classes, BS), BF16), ((8, SHARE, BS), BF16)],
        (keep, *received),
    )


def aggregate_body(
    keep_ref, r1_ref, r2_ref, r3_ref, g0_ref, g1_ref, g2_ref, g3_ref, out_ref, grad_ref
):
    out_ref[...] = four(keep_ref[...], r1_ref[...], r2_ref[...], r3_ref[...]).astype(BF16)
    for d, ref in enumerate((g0_ref, g1_ref, g2_ref, g3_ref)):
        grad_ref[4 * d : 4 * d + 4] = ref[...]


def aggregate(keep, received, cotangents):
    gathered = (16,) + cotangents[0].shape[1:]
    return call(
        aggregate_body,
        [((BS, BS), BF16), (gathered, BF16)],
        (keep, *received, *cotangents),
    )


def share_sum_body(parts_ref, out_ref):
    total = parts_ref[0].astype(F32)
    for c in range(1, 8):
        total = total + parts_ref[c].astype(F32)
    out_ref[...] = total


def share_sum(parts):
    return call(share_sum_body, [((SHARE, BS), F32)], (parts,))[0]


def unpack_body(me_ref, own_ref, r1_ref, r2_ref, r3_ref, in_ref, out_ref, all_ref):
    x = me_ref[0] // 8
    for d, ref in enumerate((own_ref, r1_ref, r2_ref, r3_ref)):
        all_ref[lax.bitwise_xor(d, x)] = ref[...]
    unit = 0
    for ref in (in_ref, out_ref):
        for side in range(2):
            for u in range(-(-ref.shape[0] // UNIT)):
                place, at = divmod(unit, UNITS)
                rows = min(UNIT, ref.shape[0] - u * UNIT)
                ref[u * UNIT : u * UNIT + rows, side * BS : (side + 1) * BS] = all_ref[
                    place, at * UNIT : at * UNIT + rows, :
                ]
                unit += 1


def unpack(me, own, received, classes):
    return call(
        unpack_body,
        [((128, 256), F32), ((classes, 256), F32)],
        (me, own, *received),
        [smem()] + [vmem()] * 4,
        [pltpu.VMEM((4, SHARE, BS), F32)],
    )


def permute(x, flip):
    return lax.ppermute(x, "row", [(i, i ^ flip) for i in range(32)])


def gather_col(x):
    far = lax.ppermute(x, "col", [(i, i ^ 4) for i in range(8)])
    pair = jnp.stack([x, far])
    return [pair] + [lax.ppermute(pair, "col", [(i, i ^ d) for i in range(8)]) for d in (1, 2, 3)]


CORE = 1
Z_FLIPS = (2, 4, 6)
X_FLIPS = (8, 16, 24)


def on_device(features, block_values, block_slots, block_counts, w_in, w_out, logit_grad):
    classes = logit_grad.shape[1]
    me = lax.axis_index("row").astype(jnp.int32).reshape(1)
    side = lax.axis_index("col").astype(jnp.int32).reshape(1)
    w_out_t = w_out.T
    parts = gather_col(features)
    grad_t = logit_grad.T
    cotangents = [grad_t] + [permute(grad_t, f) for f in Z_FLIPS]
    dense = densify(me, side, block_counts, block_slots, block_values)
    far, grad_z = rows_product_far(dense, parts, cotangents)
    got = permute(far, CORE)
    mine = rows_product_near(dense, parts)
    s1, s2, s3, keep = core_sum(mine, got)
    received = [permute(s, f) for s, f in zip((s1, s2, s3), X_FLIPS)]
    grad_x = [grad_z] + [permute(grad_z, f) for f in X_FLIPS]
    s1, s2, s3, keep = x_sum(keep, received)
    received = [permute(s, f) for s, f in zip((s1, s2, s3), Z_FLIPS)]
    agg, grad_near = aggregate(keep, received, grad_x)
    grad_far = permute(grad_near, CORE)
    agg = gather_col(agg)
    q = class_columns(grad_near, grad_far, dense)

    wide, far = class_rows_far(agg, w_in, w_out_t, q, me, dense)
    got = permute(far, CORE)
    mine = class_rows_near(wide, dense)
    s1, s2, s3, keep = core_sum_grad(mine, far, got)
    s1, s2, s3, keep = x_sum_grad(keep, [permute(s, f) for s, f in zip((s1, s2, s3), X_FLIPS)])
    received = [permute(s, f) for s, f in zip((s1, s2, s3), Z_FLIPS)]
    logits_t, shares = z_sum_grad(keep, received, classes)
    own = share_sum(lax.all_to_all(shares, "col", 0, 0))
    in_grad, out_grad_t = unpack(me, own, [permute(own, f) for f in X_FLIPS], classes)
    return (logits_t.T, in_grad, out_grad_t.T)


def solution(mesh):
    return jax.shard_map(
        on_device,
        mesh=mesh,
        in_specs=(
            P(("col", "row"), None),
            P(("row", "col"), None, None),
            P(("row", "col")),
            P(("row", "col")),
            P(),
            P(),
            P(("col", "row"), None),
        ),
        out_specs=(P(("col", "row"), None), P(), P()),
        check_vma=False,
    )
```
